32 devices in a mesh: rep: 2 (over x), feat: 16 (over z, y, core).
Axes of the slice: x: 2, y: 2, z: 4, core: 2. Of those that a mesh axis runs over, the one named last changes fastest.
Arguments:
- view_a: bfloat16 [512, 16384], P(('rep', 'feat')), parts along dimension 0, may hold values from -13 to 13
- view_b: bfloat16 [512, 16384], P(('rep', 'feat')), parts along dimension 0, may hold values from -13 to 13
Outputs:
- grad_a: bfloat16 [512, 16384], P(('rep', 'feat')), parts along dimension 0
- grad_b: bfloat16 [512, 16384], P(('rep', 'feat')), parts along dimension 0
The draws below stay inside these ranges and needn't reach their ends.
There are 2 independent parts, one for each index of `rep`. The reference program is written for one: setup_inputs(seed, part) draws one part's arguments, and reference() takes and returns one part's arrays. A program takes and returns all parts, laid end to end along the dimension named above; each array names one. Nothing has to cross between parts.
All inputs are finite; a program needn't handle non-finite values.
Results may differ from the reference program's by a relative error of at most 0.007.
Values may be sent and summed in bfloat16 or wider, within the bound.
A program may use at most 64 MiB of HBM per device.

```python
import jax
import jax.numpy as jnp
from jax import lax

F = 16384
B = 256


def shared_base(key):
    normal_part = jax.random.truncated_normal(key, -4.0, 4.0, (B, F), jnp.float32)
    return normal_part


def common_part(key):
    count = max(F // 1024, 1)
    key_z, key_m, key_t = jax.random.split(key, 3)
    factors = jax.random.truncated_normal(key_z, -3.0, 3.0, (B, count), jnp.float32)
    mixing = jax.random.truncated_normal(key_m, -3.0, 3.0, (count, F), jnp.float32) / jnp.sqrt(jnp.float32(count))
    summed = jnp.zeros((B, F), jnp.float32)
    for index in range(count):
        summed = summed + factors[:, index:index + 1] * mixing[index:index + 1, :]
    position = jnp.arange(F, dtype=jnp.float32)[None, :] / F
    jitter = jnp.exp(jax.random.uniform(key_t, (1, F), jnp.float32, jnp.log(0.8), jnp.log(1.25)))
    return summed * ((0.35 + 0.35 * position) * jitter)


def feature_law(key, low, high):
    first, second = jax.random.split(key)
    scales = jnp.exp(jax.random.uniform(first, (1, F), jnp.float32, jnp.log(low), jnp.log(high)))
    offsets = jax.random.uniform(second, (1, F), jnp.float32, -1.0, 1.0)
    return (scales, offsets)


def draw_view_a(key, part):
    base = shared_base(key)
    common = common_part(jax.random.fold_in(key, 41))
    key = jax.random.fold_in(key, 11)
    scales, offsets = feature_law(key, 0.5, 2.0)
    return jnp.clip((base + common) * scales + offsets, -13.0, 13.0).astype(jnp.bfloat16)


def draw_view_b(key, part):
    base = shared_base(key)
    common = common_part(jax.random.fold_in(key, 41))
    key = jax.random.fold_in(key, 23)
    noise = jax.random.truncated_normal(jax.random.fold_in(key, 3), -4.0, 4.0, (B, F), jnp.float32)
    scales, offsets = feature_law(key, 0.5, 2.0)
    mixed = 0.8 * base + 0.6 * noise
    return jnp.clip((mixed + common) * scales + offsets, -13.0, 13.0).astype(jnp.bfloat16)


def setup_inputs(seed: int = 0, part: int = 0) -> dict:
    key_list = jax.random.split(jax.random.key(seed), 3)
    own_keys = jax.random.split(jax.random.fold_in(key_list[2], part), 3)
    view_a = draw_view_a(jax.random.fold_in(jax.random.fold_in(key_list[2], part), 71), part)
    view_b = draw_view_b(jax.random.fold_in(jax.random.fold_in(key_list[2], part), 71), part)
    return dict(view_a=view_a, view_b=view_b)


LAMBDA = 0.0051

def normalize(values):
    floats = values.astype(jnp.float32)
    center = lax.optimization_barrier(jnp.mean(floats, axis=0, keepdims=True))
    spread = lax.optimization_barrier(jnp.mean((floats - center) ** 2, axis=0, keepdims=True))
    inverse = lax.rsqrt(spread + 1e-05)
    return (((floats - center) * inverse).astype(jnp.bfloat16), inverse)

def backward(dnorm, normed, inverse):
    floats = normed.astype(jnp.float32)
    mean_d = lax.optimization_barrier(jnp.mean(dnorm, axis=0, keepdims=True))
    mean_p = lax.optimization_barrier(jnp.mean(dnorm * floats, axis=0, keepdims=True))
    return ((dnorm - mean_d - floats * mean_p) * inverse).astype(jnp.bfloat16)

def inner_matrix(normed):
    return lax.dot_general(normed, normed, (((1,), (1,)), ((), ())), preferred_element_type=jnp.float32)

def reference(view_a, view_b):
    norm_a, inv_a = normalize(view_a)
    norm_b, inv_b = normalize(view_b)
    images = norm_a.shape[0]
    diag_corr = lax.optimization_barrier(jnp.sum(norm_a.astype(jnp.float32) * norm_b.astype(jnp.float32), axis=0, keepdims=True)) / images
    self_weight = -2.0 * (1.0 - diag_corr) - 2.0 * LAMBDA * diag_corr
    factor = 2.0 * LAMBDA / images
    mix_a = (inner_matrix(norm_a) * factor).astype(jnp.bfloat16)
    mix_b = (inner_matrix(norm_b) * factor).astype(jnp.bfloat16)
    dnorm_a = jnp.dot(mix_b, norm_a, preferred_element_type=jnp.float32) + norm_b.astype(jnp.float32) * self_weight
    dnorm_b = jnp.dot(mix_a, norm_b, preferred_element_type=jnp.float32) + norm_a.astype(jnp.float32) * self_weight
    return (backward(dnorm_a, norm_a, inv_a), backward(dnorm_b, norm_b, inv_b))
```

```python
import functools

import jax
import jax.numpy as jnp
from jax import lax
from jax.experimental import pallas as pl
from jax.experimental.pallas import tpu as pltpu
from jax.sharding import PartitionSpec as P

LAMBDA = 0.0051
CHUNKS = 2


def kernel(n, chunks, view_a, view_b, out_a, out_b,
           recv, norm, inv, weight, part, terms, mix, grad,
           in_send, in_recv, own_sem, rs_send, rs_recv, ag_send, ag_recv, out_send, out_recv):
    me = lax.axis_index("feat")
    views, outs = (view_a, view_b), (out_a, out_b)
    rows, features = view_a.shape
    images = rows * n
    width = features // n
    step = width // chunks
    far = n // 2

    def my_rows(index):
        return pl.ds(pl.multiple_of(index * rows, rows), rows)

    def columns(index, chunk):
        return pl.ds(pl.multiple_of(index * width + chunk * step, 128), step)

    def each_peer(visit):
        def at(j, carry):
            offset = far + (j + 1) // 2 * (1 - 2 * (j % 2))
            visit(offset, lax.rem(me + offset, n))
            return carry
        lax.fori_loop(0, n - 1, at, 0)

    def push(src, dst, send, receive, peer):
        pltpu.make_async_remote_copy(
            src_ref=src, dst_ref=dst, send_sem=send, recv_sem=receive,
            device_id={"feat": peer}, device_id_type=pl.DeviceIdType.MESH,
        ).start()

    def await_bytes(ref, sem):
        pltpu.make_async_copy(ref, ref, sem).wait()

    barrier = pltpu.get_barrier_semaphore()
    each_peer(lambda offset, peer: pl.semaphore_signal(
        barrier, inc=1, device_id={"feat": peer}, device_id_type=pl.DeviceIdType.MESH))
    own = [[pltpu.make_async_copy(views[v].at[:, columns(me, c)], recv.at[v, c, my_rows(me)], own_sem.at[v, c])
            for c in range(chunks)] for v in range(2)]
    for v in range(2):
        for c in range(chunks):
            own[v][c].start()
    pl.semaphore_wait(barrier, n - 1)

    for v in range(2):
        for c in range(chunks):
            each_peer(lambda offset, peer: push(
                views[v].at[:, columns(peer, c)], recv.at[v, c, my_rows(me)],
                in_send.at[v, c], in_recv.at[v, c], peer))

    def normalize(v, c):
        own[v][c].wait()
        await_bytes(recv.at[v, c, pl.ds(0, images - rows)], in_recv.at[v, c])
        floats = recv[v, c].astype(jnp.float32)
        center = jnp.mean(floats, axis=0, keepdims=True)
        shifted = floats - center
        spread = jnp.mean(shifted * shifted, axis=0, keepdims=True)
        inverse = lax.rsqrt(spread + 1e-05)
        inv[v, c] = inverse
        norm[v, c] = (shifted * inverse).astype(jnp.bfloat16)

    def inner(v):
        total = None
        for c in range(chunks):
            term = lax.dot_general(norm[v, c], norm[v, c], (((1,), (1,)), ((), ())),
                                   preferred_element_type=jnp.float32)
            total = term if total is None else total + term
        part[v] = total.astype(jnp.bfloat16)
        each_peer(lambda offset, peer: push(
            part.at[v, my_rows(peer)], terms.at[v, offset - 1], rs_send.at[v], rs_recv.at[v], peer))

    def reduce(v):
        await_bytes(terms.at[v], rs_recv.at[v])
        total = part[v, my_rows(me)].astype(jnp.float32)
        for k in range(n - 1):
            total = total + terms[v, k].astype(jnp.float32)
        factor = 2.0 * LAMBDA / images
        mix[v, my_rows(me)] = (total * factor).astype(jnp.bfloat16)
        each_peer(lambda offset, peer: push(
            mix.at[v, my_rows(me)], mix.at[v, my_rows(me)], ag_send.at[v], ag_recv.at[v], peer))

    def self_weight(c):
        first, second = norm[0, c].astype(jnp.float32), norm[1, c].astype(jnp.float32)
        diagonal = jnp.sum(first * second, axis=0, keepdims=True) / images
        weight[c] = -2.0 * (1.0 - diagonal) - 2.0 * LAMBDA * diagonal

    def await_mix(v):
        await_bytes(mix.at[v, pl.ds(0, images - rows)], ag_recv.at[v])

    def backward(v, c):
        floats = norm[v, c].astype(jnp.float32)
        dnorm = jnp.dot(mix[1 - v], norm[v, c], preferred_element_type=jnp.float32)
        dnorm = dnorm + norm[1 - v, c].astype(jnp.float32) * weight[c]
        mean_d = jnp.mean(dnorm, axis=0, keepdims=True)
        mean_p = jnp.mean(dnorm * floats, axis=0, keepdims=True)
        grad[v, c] = ((dnorm - mean_d - floats * mean_p) * inv[v, c]).astype(jnp.bfloat16)
        each_peer(lambda offset, peer: push(
            grad.at[v, c, my_rows(peer)], outs[v].at[:, columns(me, c)],
            out_send.at[v, c], out_recv.at[v, c], peer))
        copy = pltpu.make_async_copy(grad.at[v, c, my_rows(me)], outs[v].at[:, columns(me, c)], own_sem.at[v, c])
        copy.start()
        return copy

    for c in range(chunks):
        normalize(0, c)
    inner(0)
    copies = []
    for c in range(chunks):
        normalize(1, c)
        self_weight(c)
        if c == 0:
            reduce(0)
    inner(1)
    await_mix(0)
    for c in range(chunks):
        copies.append(backward(1, c))
        if c == 0:
            reduce(1)
    await_mix(1)
    for c in range(chunks):
        copies.append(backward(0, c))

    for copy in copies:
        copy.wait()
    for v in range(2):
        await_bytes(terms.at[v], rs_send.at[v])
        await_bytes(mix.at[v, pl.ds(0, images - rows)], ag_send.at[v])
        for c in range(chunks):
            await_bytes(recv.at[v, c, pl.ds(0, images - rows)], in_send.at[v, c])
            await_bytes(grad.at[v, c, pl.ds(0, images - rows)], out_send.at[v, c])
            await_bytes(grad.at[v, c, pl.ds(0, images - rows)], out_recv.at[v, c])


def body(n, view_a, view_b):
    rows, features = view_a.shape
    images, width = rows * n, features // n
    chunks = CHUNKS
    while width % (chunks * 128):
        chunks -= 1
    step = width // chunks
    half = jnp.bfloat16
    blocks = (2, chunks, images, step)
    return pl.pallas_call(
        functools.partial(kernel, n, chunks),
        out_shape=[jax.ShapeDtypeStruct(view_a.shape, half)] * 2,
        in_specs=[pl.BlockSpec(memory_space=pl.ANY)] * 2,
        out_specs=[pl.BlockSpec(memory_space=pl.ANY)] * 2,
        scratch_shapes=[
            pltpu.VMEM(blocks, half),
            pltpu.VMEM(blocks, half),
            pltpu.VMEM((2, chunks, 1, step), jnp.float32),
            pltpu.VMEM((chunks, 1, step), jnp.float32),
            pltpu.VMEM((2, images, images), half),
            pltpu.VMEM((2, n - 1, rows, images), half),
            pltpu.VMEM((2, images, images), half),
            pltpu.VMEM(blocks, half),
            pltpu.SemaphoreType.DMA((2, chunks)),
            pltpu.SemaphoreType.DMA((2, chunks)),
            pltpu.SemaphoreType.DMA((2, chunks)),
            pltpu.SemaphoreType.DMA((2,)),
            pltpu.SemaphoreType.DMA((2,)),
            pltpu.SemaphoreType.DMA((2,)),
            pltpu.SemaphoreType.DMA((2,)),
            pltpu.SemaphoreType.DMA((2, chunks)),
            pltpu.SemaphoreType.DMA((2, chunks)),
        ],
        compiler_params=pltpu.CompilerParams(
            collective_id=0, has_side_effects=True, vmem_limit_bytes=48 * 1024 * 1024),
        cost_estimate=pl.CostEstimate(
            flops=8 * images * images * width, bytes_accessed=8 * rows * features, transcendentals=2 * width),
    )(view_a, view_b)


def solution(mesh):
    placed = (P(("rep", "feat"), None), P(("rep", "feat"), None))
    return jax.shard_map(
        functools.partial(body, mesh.shape["feat"]),
        mesh=mesh,
        in_specs=placed,
        out_specs=placed,
        check_vma=False,
    )
```

```python
import functools

import jax
import jax.numpy as jnp
from jax import lax
from jax.experimental import pallas as pl
from jax.experimental.pallas import tpu as pltpu
from jax.sharding import PartitionSpec as P

LAMBDA = 0.0051
CHUNKS = 2


def kernel(n, chunks, view_a, view_b, out_a, out_b,
           recv, norm, inv, weight, part, terms, summed, sent, crossed, mix, grad,
           in_send, in_recv, own_sem, rs_send, rs_recv, cross_send, cross_recv, ag_send, ag_recv, out_send, out_recv):
    me = lax.axis_index("feat")
    views, outs = (view_a, view_b), (out_a, out_b)
    rows, features = view_a.shape
    images = rows * n
    width = features // n
    step = width // chunks
    half = n // 2
    owned = images // half
    place = lax.rem(me, half)
    base = me - place
    mirror = lax.rem(me + half, n)

    def my_rows(index):
        return pl.ds(pl.multiple_of(index * rows, rows), rows)

    def columns(index, chunk):
        return pl.ds(pl.multiple_of(index * width + chunk * step, 128), step)

    def owned_rows(index):
        return pl.ds(pl.multiple_of(index * owned, owned), owned)

    def each_peer(visit, group=None):
        def at(j, carry):
            offset = j if group is None else 2 * j + 1 + group
            visit(offset, lax.rem(me + offset, n))
            return carry
        if group is None:
            lax.fori_loop(1, n, at, 0)
        else:
            lax.fori_loop(0, half - group, at, 0)

    def each_near(visit):
        def at(offset, carry):
            visit(offset, lax.rem(place + offset, half))
            return carry
        lax.fori_loop(1, half, at, 0)

    def push(src, dst, send, receive, peer):
        pltpu.make_async_remote_copy(
            src_ref=src, dst_ref=dst, send_sem=send, recv_sem=receive,
            device_id={"feat": peer}, device_id_type=pl.DeviceIdType.MESH,
        ).start()

    def await_bytes(ref, sem):
        pltpu.make_async_copy(ref, ref, sem).wait()

    barrier = pltpu.get_barrier_semaphore()
    each_peer(lambda offset, peer: pl.semaphore_signal(
        barrier, inc=1, device_id={"feat": peer}, device_id_type=pl.DeviceIdType.MESH))
    own = [[pltpu.make_async_copy(views[v].at[:, columns(me, c)], recv.at[v, c, my_rows(me)], own_sem.at[v, c])
            for c in range(chunks)] for v in range(2)]
    for v in range(2):
        for c in range(chunks):
            own[v][c].start()
    pl.semaphore_wait(barrier, n - 1)

    def send_view(v, c, group=None):
        each_peer(lambda offset, peer: push(
            views[v].at[:, columns(peer, c)], recv.at[v, c, my_rows(me)],
            in_send.at[v, c], in_recv.at[v, c], peer), group)

    def send_grad(v, c, group=None):
        each_peer(lambda offset, peer: push(
            grad.at[v, c, my_rows(peer)], outs[v].at[:, columns(me, c)],
            out_send.at[v, c], out_recv.at[v, c], peer), group)

    def normalize(v, c):
        own[v][c].wait()
        await_bytes(recv.at[v, c, pl.ds(0, images - rows)], in_recv.at[v, c])
        floats = recv[v, c].astype(jnp.float32)
        center = jnp.mean(floats, axis=0, keepdims=True)
        shifted = floats - center
        spread = jnp.mean(shifted * shifted, axis=0, keepdims=True)
        inverse = lax.rsqrt(spread + 1e-05)
        inv[v, c] = inverse
        norm[v, c] = (shifted * inverse).astype(jnp.bfloat16)

    def inner(v):
        total = None
        for c in range(chunks):
            term = lax.dot_general(norm[v, c], norm[v, c], (((1,), (1,)), ((), ())),
                                   preferred_element_type=jnp.float32)
            total = term if total is None else total + term
        part[v] = total.astype(jnp.bfloat16)
        each_near(lambda offset, other: push(
            part.at[v, owned_rows(other)], terms.at[v, offset - 1], rs_send.at[v], rs_recv.at[v], base + other))

    def reduce(v):
        await_bytes(terms.at[v], rs_recv.at[v])
        total = part[v, owned_rows(place)].astype(jnp.float32)
        for k in range(half - 1):
            total = total + terms[v, k].astype(jnp.float32)
        summed[v] = total
        sent[v] = total.astype(jnp.bfloat16)
        push(sent.at[v], crossed.at[v], cross_send.at[v], cross_recv.at[v], mirror)

    def finish(v):
        await_bytes(crossed.at[v], cross_recv.at[v])
        total = summed[v] + crossed[v].astype(jnp.float32)
        factor = 2.0 * LAMBDA / images
        mix[v, owned_rows(place)] = (total * factor).astype(jnp.bfloat16)
        each_near(lambda offset, other: push(
            mix.at[v, owned_rows(place)], mix.at[v, owned_rows(place)], ag_send.at[v], ag_recv.at[v], base + other))

    def self_weight(c):
        first, second = norm[0, c].astype(jnp.float32), norm[1, c].astype(jnp.float32)
        diagonal = jnp.sum(first * second, axis=0, keepdims=True) / images
        weight[c] = -2.0 * (1.0 - diagonal) - 2.0 * LAMBDA * diagonal

    def await_mix(v):
        await_bytes(mix.at[v, pl.ds(0, images - owned)], ag_recv.at[v])

    def backward(v, c):
        floats = norm[v, c].astype(jnp.float32)
        dnorm = jnp.dot(mix[1 - v], norm[v, c], preferred_element_type=jnp.float32)
        dnorm = dnorm + norm[1 - v, c].astype(jnp.float32) * weight[c]
        mean_d = jnp.mean(dnorm, axis=0, keepdims=True)
        mean_p = jnp.mean(dnorm * floats, axis=0, keepdims=True)
        grad[v, c] = ((dnorm - mean_d - floats * mean_p) * inv[v, c]).astype(jnp.bfloat16)
        copy = pltpu.make_async_copy(grad.at[v, c, my_rows(me)], outs[v].at[:, columns(me, c)], own_sem.at[v, c])
        copy.start()
        return copy

    view_groups = [(c, group) for c in range(chunks) for group in range(2)]
    for c in range(chunks):
        send_view(0, c)
    send_view(1, *view_groups[0])
    for c in range(chunks):
        normalize(0, c)
    inner(0)
    send_view(1, *view_groups[1])
    reduce(0)
    for group in view_groups[2:3]:
        send_view(1, *group)
    finish(0)
    for group in view_groups[3:]:
        send_view(1, *group)
    normalize(1, 0)
    self_weight(0)
    await_mix(0)
    copies = [backward(1, 0)]
    send_grad(1, 0, 0)
    for c in range(1, chunks):
        normalize(1, c)
        self_weight(c)
    inner(1)
    send_grad(1, 0, 1)
    for c in range(1, chunks):
        copies.append(backward(1, c))
    reduce(1)
    for c in range(1, chunks):
        send_grad(1, c, 0)
    finish(1)
    for c in range(1, chunks):
        send_grad(1, c, 1)
    await_mix(1)
    for c in range(chunks):
        copies.append(backward(0, c))
        send_grad(0, c)

    for copy in copies:
        copy.wait()
    for v in range(2):
        await_bytes(terms.at[v], rs_send.at[v])
        await_bytes(sent.at[v], cross_send.at[v])
        await_bytes(mix.at[v, pl.ds(0, images - owned)], ag_send.at[v])
        for c in range(chunks):
            await_bytes(recv.at[v, c, pl.ds(0, images - rows)], in_send.at[v, c])
            await_bytes(grad.at[v, c, pl.ds(0, images - rows)], out_send.at[v, c])
            await_bytes(grad.at[v, c, pl.ds(0, images - rows)], out_recv.at[v, c])


def body(n, view_a, view_b):
    rows, features = view_a.shape
    images, width = rows * n, features // n
    chunks = CHUNKS
    while width % (chunks * 128):
        chunks -= 1
    step = width // chunks
    half = jnp.bfloat16
    blocks = (2, chunks, images, step)
    return pl.pallas_call(
        functools.partial(kernel, n, chunks),
        out_shape=[jax.ShapeDtypeStruct(view_a.shape, half)] * 2,
        in_specs=[pl.BlockSpec(memory_space=pltpu.HBM)] * 2,
        out_specs=[pl.BlockSpec(memory_space=pl.ANY)] * 2,
        scratch_shapes=[
            pltpu.VMEM(blocks, half),
            pltpu.VMEM(blocks, half),
            pltpu.VMEM((2, chunks, 1, step), jnp.float32),
            pltpu.VMEM((chunks, 1, step), jnp.float32),
            pltpu.VMEM((2, images, images), half),
            pltpu.VMEM((2, n // 2 - 1, 2 * rows, images), half),
            pltpu.VMEM((2, 2 * rows, images), jnp.float32),
            pltpu.VMEM((2, 2 * rows, images), half),
            pltpu.VMEM((2, 2 * rows, images), half),
            pltpu.VMEM((2, images, images), half),
            pltpu.VMEM(blocks, half),
            pltpu.SemaphoreType.DMA((2, chunks)),
            pltpu.SemaphoreType.DMA((2, chunks)),
            pltpu.SemaphoreType.DMA((2, chunks)),
            pltpu.SemaphoreType.DMA((2,)),
            pltpu.SemaphoreType.DMA((2,)),
            pltpu.SemaphoreType.DMA((2,)),
            pltpu.SemaphoreType.DMA((2,)),
            pltpu.SemaphoreType.DMA((2,)),
            pltpu.SemaphoreType.DMA((2,)),
            pltpu.SemaphoreType.DMA((2, chunks)),
            pltpu.SemaphoreType.DMA((2, chunks)),
        ],
        compiler_params=pltpu.CompilerParams(
            collective_id=0, has_side_effects=True, vmem_limit_bytes=48 * 1024 * 1024),
        cost_estimate=pl.CostEstimate(
            flops=8 * images * images * width, bytes_accessed=8 * rows * features, transcendentals=2 * width),
    )(view_a, view_b)


def solution(mesh):
    placed = (P(("rep", "feat"), None), P(("rep", "feat"), None))
    return jax.shard_map(
        functools.partial(body, mesh.shape["feat"]),
        mesh=mesh,
        in_specs=placed,
        out_specs=placed,
        check_vma=False,
    )
```

```python
import functools

import jax
import jax.numpy as jnp
from jax import lax
from jax.experimental import pallas as pl
from jax.experimental.pallas import tpu as pltpu
from jax.sharding import PartitionSpec as P

LAMBDA = 0.0051
CHUNKS = 2
GROUPS = 4


def kernel(n, chunks, view_a, view_b, out_a, out_b,
           recv, norm, inv, weight, gram, part, terms, summed, sent, crossed, mix, grad,
           in_send, in_recv, own_sem, rs_send, rs_recv, cross_send, cross_recv, ag_send, ag_recv, out_send, out_recv):
    me = lax.axis_index("feat")
    views, outs = (view_a, view_b), (out_a, out_b)
    rows, features = view_a.shape
    images = rows * n
    width = features // n
    step = width // chunks
    half = n // 2
    owned = images // half
    place = lax.rem(me, half)
    base = me - place
    mirror = lax.rem(me + half, n)

    def my_rows(index):
        return pl.ds(pl.multiple_of(index * rows, rows), rows)

    def columns(index, chunk):
        return pl.ds(pl.multiple_of(index * width + chunk * step, 128), step)

    def owned_rows(index):
        return pl.ds(pl.multiple_of(index * owned, owned), owned)

    def each_peer(visit, group=None):
        def at(j, carry):
            offset = j if group is None else GROUPS * j + 1 + group
            visit(offset, lax.rem(me + offset, n))
            return carry
        if group is None:
            lax.fori_loop(1, n, at, 0)
        else:
            lax.fori_loop(0, (n - 1 - group + GROUPS - 1) // GROUPS, at, 0)

    def each_near(visit):
        def at(offset, carry):
            visit(offset, lax.rem(place + offset, half))
            return carry
        lax.fori_loop(1, half, at, 0)

    def push(src, dst, send, receive, peer):
        pltpu.make_async_remote_copy(
            src_ref=src, dst_ref=dst, send_sem=send, recv_sem=receive,
            device_id={"feat": peer}, device_id_type=pl.DeviceIdType.MESH,
        ).start()

    def await_bytes(ref, sem):
        pltpu.make_async_copy(ref, ref, sem).wait()

    barrier = pltpu.get_barrier_semaphore()
    each_peer(lambda offset, peer: pl.semaphore_signal(
        barrier, inc=1, device_id={"feat": peer}, device_id_type=pl.DeviceIdType.MESH))
    own = [[pltpu.make_async_copy(views[v].at[:, columns(me, c)], recv.at[v, c, my_rows(me)], own_sem.at[v, c])
            for c in range(chunks)] for v in range(2)]
    for v in range(2):
        for c in range(chunks):
            own[v][c].start()
    pl.semaphore_wait(barrier, n - 1)

    def send_view(v, c, group=None):
        each_peer(lambda offset, peer: push(
            views[v].at[:, columns(peer, c)], recv.at[v, c, my_rows(me)],
            in_send.at[v, c], in_recv.at[v, c], peer), group)

    def send_grad(v, c, group=None):
        each_peer(lambda offset, peer: push(
            grad.at[v, c, my_rows(peer)], outs[v].at[:, columns(me, c)],
            out_send.at[v, c], out_recv.at[v, c], peer), group)

    def normalize(v, c):
        own[v][c].wait()
        await_bytes(recv.at[v, c, pl.ds(0, images - rows)], in_recv.at[v, c])
        floats = recv[v, c].astype(jnp.float32)
        center = jnp.mean(floats, axis=0, keepdims=True)
        shifted = floats - center
        spread = jnp.mean(shifted * shifted, axis=0, keepdims=True)
        inverse = lax.rsqrt(spread + 1e-05)
        inv[v, c] = inverse
        norm[v, c] = (shifted * inverse).astype(jnp.bfloat16)

    def inner(v, c):
        term = lax.dot_general(norm[v, c], norm[v, c], (((1,), (1,)), ((), ())), preferred_element_type=jnp.float32)
        if c:
            term = gram[...] + term
        if c < chunks - 1:
            gram[...] = term
            return
        part[v] = term.astype(jnp.bfloat16)
        each_near(lambda offset, other: push(
            part.at[v, owned_rows(other)], terms.at[v, offset - 1], rs_send.at[v], rs_recv.at[v], base + other))

    def reduce(v):
        await_bytes(terms.at[v], rs_recv.at[v])
        total = part[v, owned_rows(place)].astype(jnp.float32)
        for k in range(half - 1):
            total = total + terms[v, k].astype(jnp.float32)
        summed[v] = total
        sent[v] = total.astype(jnp.bfloat16)
        push(sent.at[v], crossed.at[v], cross_send.at[v], cross_recv.at[v], mirror)

    def finish(v):
        await_bytes(crossed.at[v], cross_recv.at[v])
        total = summed[v] + crossed[v].astype(jnp.float32)
        factor = 2.0 * LAMBDA / images
        mix[v, owned_rows(place)] = (total * factor).astype(jnp.bfloat16)
        each_near(lambda offset, other: push(
            mix.at[v, owned_rows(place)], mix.at[v, owned_rows(place)], ag_send.at[v], ag_recv.at[v], base + other))

    def self_weight(c):
        first, second = norm[0, c].astype(jnp.float32), norm[1, c].astype(jnp.float32)
        diagonal = jnp.sum(first * second, axis=0, keepdims=True) / images
        weight[c] = -2.0 * (1.0 - diagonal) - 2.0 * LAMBDA * diagonal

    def await_mix(v):
        await_bytes(mix.at[v, pl.ds(0, images - owned)], ag_recv.at[v])

    def backward(v, c):
        floats = norm[v, c].astype(jnp.float32)
        dnorm = jnp.dot(mix[1 - v], norm[v, c], preferred_element_type=jnp.float32)
        dnorm = dnorm + norm[1 - v, c].astype(jnp.float32) * weight[c]
        mean_d = jnp.mean(dnorm, axis=0, keepdims=True)
        mean_p = jnp.mean(dnorm * floats, axis=0, keepdims=True)
        grad[v, c] = ((dnorm - mean_d - floats * mean_p) * inv[v, c]).astype(jnp.bfloat16)
        copy = pltpu.make_async_copy(grad.at[v, c, my_rows(me)], outs[v].at[:, columns(me, c)], own_sem.at[v, c])
        copy.start()
        return copy

    copies = []
    send_view(0, 0)
    send_view(0, 1)
    send_view(1, 0, 0)
    send_view(1, 0, 1)
    normalize(0, 0)
    inner(0, 0)
    normalize(0, 1)
    inner(0, 1)
    send_view(1, 0, 2)
    send_view(1, 0, 3)
    send_view(1, 1, 0)
    reduce(0)
    send_view(1, 1, 1)
    send_view(1, 1, 2)
    finish(0)
    send_view(1, 1, 3)
    normalize(1, 0)
    inner(1, 0)
    self_weight(0)
    await_mix(0)
    copies.append(backward(1, 0))
    send_grad(1, 0, 0)
    normalize(1, 1)
    self_weight(1)
    inner(1, 1)
    send_grad(1, 0, 1)
    send_grad(1, 0, 2)
    reduce(1)
    send_grad(1, 0, 3)
    copies.append(backward(1, 1))
    send_grad(1, 1, 0)
    finish(1)
    send_grad(1, 1, 1)
    send_grad(1, 1, 2)
    send_grad(1, 1, 3)
    await_mix(1)
    for c in range(chunks):
        copies.append(backward(0, c))
        send_grad(0, c)

    for copy in copies:
        copy.wait()
    for v in range(2):
        await_bytes(terms.at[v], rs_send.at[v])
        await_bytes(sent.at[v], cross_send.at[v])
        await_bytes(mix.at[v, pl.ds(0, images - owned)], ag_send.at[v])
        for c in range(chunks):
            await_bytes(recv.at[v, c, pl.ds(0, images - rows)], in_send.at[v, c])
            await_bytes(grad.at[v, c, pl.ds(0, images - rows)], out_send.at[v, c])
            await_bytes(grad.at[v, c, pl.ds(0, images - rows)], out_recv.at[v, c])


def body(n, view_a, view_b):
    rows, features = view_a.shape
    images, width = rows * n, features // n
    chunks = CHUNKS
    while width % (chunks * 128):
        chunks -= 1
    step = width // chunks
    half = jnp.bfloat16
    blocks = (2, chunks, images, step)
    return pl.pallas_call(
        functools.partial(kernel, n, chunks),
        out_shape=[jax.ShapeDtypeStruct(view_a.shape, half)] * 2,
        in_specs=[pl.BlockSpec(memory_space=pltpu.HBM)] * 2,
        out_specs=[pl.BlockSpec(memory_space=pl.ANY)] * 2,
        scratch_shapes=[
            pltpu.VMEM(blocks, half),
            pltpu.VMEM(blocks, half),
            pltpu.VMEM((2, chunks, 1, step), jnp.float32),
            pltpu.VMEM((chunks, 1, step), jnp.float32),
            pltpu.VMEM((images, images), jnp.float32),
            pltpu.VMEM((2, images, images), half),
            pltpu.VMEM((2, n // 2 - 1, 2 * rows, images), half),
            pltpu.VMEM((2, 2 * rows, images), jnp.float32),
            pltpu.VMEM((2, 2 * rows, images), half),
            pltpu.VMEM((2, 2 * rows, images), half),
            pltpu.VMEM((2, images, images), half),
            pltpu.VMEM(blocks, half),
            pltpu.SemaphoreType.DMA((2, chunks)),
            pltpu.SemaphoreType.DMA((2, chunks)),
            pltpu.SemaphoreType.DMA((2, chunks)),
            pltpu.SemaphoreType.DMA((2,)),
            pltpu.SemaphoreType.DMA((2,)),
            pltpu.SemaphoreType.DMA((2,)),
            pltpu.SemaphoreType.DMA((2,)),
            pltpu.SemaphoreType.DMA((2,)),
            pltpu.SemaphoreType.DMA((2,)),
            pltpu.SemaphoreType.DMA((2, chunks)),
            pltpu.SemaphoreType.DMA((2, chunks)),
        ],
        compiler_params=pltpu.CompilerParams(
            collective_id=0, has_side_effects=True, vmem_limit_bytes=48 * 1024 * 1024),
        cost_estimate=pl.CostEstimate(
            flops=8 * images * images * width, bytes_accessed=8 * rows * features, transcendentals=2 * width),
    )(view_a, view_b)


def solution(mesh):
    placed = (P(("rep", "feat"), None), P(("rep", "feat"), None))
    return jax.shard_map(
        functools.partial(body, mesh.shape["feat"]),
        mesh=mesh,
        in_specs=placed,
        out_specs=placed,
        check_vma=False,
    )
```

```python
import functools

import jax
import jax.numpy as jnp
from jax import lax
from jax.experimental import pallas as pl
from jax.experimental.pallas import tpu as pltpu
from jax.sharding import PartitionSpec as P

LAMBDA = 0.0051
CHUNKS = 2
GROUPS = 4


def kernel(n, chunks, view_a, view_b, out_a, out_b,
           recv, norm, inv, weight, gram, part, terms, summed, sent, crossed, mix, grad,
           in_send, in_recv, own_sem, rs_send, rs_recv, cross_send, cross_recv, ag_send, ag_recv, out_send, out_recv):
    me = lax.axis_index("feat")
    views, outs = (view_a, view_b), (out_a, out_b)
    rows, features = view_a.shape
    images = rows * n
    width = features // n
    step = width // chunks
    half = n // 2
    owned = images // half
    place = lax.rem(me, half)
    base = me - place
    mirror = lax.rem(me + half, n)

    def my_rows(index):
        return pl.ds(pl.multiple_of(index * rows, rows), rows)

    def columns(index, chunk):
        return pl.ds(pl.multiple_of(index * width + chunk * step, 128), step)

    def owned_rows(index):
        return pl.ds(pl.multiple_of(index * owned, owned), owned)

    def each_peer(visit, group=None):
        def at(j, carry):
            offset = j if group is None else GROUPS * j + 1 + group
            visit(offset, lax.rem(me + offset, n))
            return carry
        if group is None:
            lax.fori_loop(1, n, at, 0)
        else:
            lax.fori_loop(0, (n - 1 - group + GROUPS - 1) // GROUPS, at, 0)

    def each_near(visit):
        def at(offset, carry):
            visit(offset, lax.rem(place + offset, half))
            return carry
        lax.fori_loop(1, half, at, 0)

    def push(src, dst, send, receive, peer):
        pltpu.make_async_remote_copy(
            src_ref=src, dst_ref=dst, send_sem=send, recv_sem=receive,
            device_id={"feat": peer}, device_id_type=pl.DeviceIdType.MESH,
        ).start()

    def await_bytes(ref, sem):
        pltpu.make_async_copy(ref, ref, sem).wait()

    barrier = pltpu.get_barrier_semaphore()
    each_peer(lambda offset, peer: pl.semaphore_signal(
        barrier, inc=1, device_id={"feat": peer}, device_id_type=pl.DeviceIdType.MESH))
    own = [[pltpu.make_async_copy(views[v].at[:, columns(me, c)], recv.at[v, c, my_rows(me)], own_sem.at[v, c])
            for c in range(chunks)] for v in range(2)]
    for v in range(2):
        for c in range(chunks):
            own[v][c].start()
    pl.semaphore_wait(barrier, n - 1)

    def send_view(v, c, group=None):
        each_peer(lambda offset, peer: push(
            views[v].at[:, columns(peer, c)], recv.at[v, c, my_rows(me)],
            in_send.at[v, c], in_recv.at[v, c], peer), group)

    def send_grad(v, c, group=None):
        each_peer(lambda offset, peer: push(
            grad.at[v, c, my_rows(peer)], outs[v].at[:, columns(me, c)],
            out_send.at[v, c], out_recv.at[v, c], peer), group)

    def normalize(v, c):
        own[v][c].wait()
        await_bytes(recv.at[v, c, pl.ds(0, images - rows)], in_recv.at[v, c])
        floats = recv[v, c].astype(jnp.float32)
        center = jnp.mean(floats, axis=0, keepdims=True)
        shifted = floats - center
        spread = jnp.mean(shifted * shifted, axis=0, keepdims=True)
        inverse = lax.rsqrt(spread + 1e-05)
        inv[v, c] = inverse
        norm[v, c] = (shifted * inverse).astype(jnp.bfloat16)

    def inner(v, c):
        term = lax.dot_general(norm[v, c], norm[v, c], (((1,), (1,)), ((), ())), preferred_element_type=jnp.float32)
        if c:
            term = gram[...] + term
        if c < chunks - 1:
            gram[...] = term
            return
        part[v] = term.astype(jnp.bfloat16)
        each_near(lambda offset, other: push(
            part.at[v, owned_rows(other)], terms.at[v, offset - 1], rs_send.at[v], rs_recv.at[v], base + other))

    def reduce(v):
        await_bytes(terms.at[v], rs_recv.at[v])
        total = part[v, owned_rows(place)].astype(jnp.float32)
        for k in range(half - 1):
            total = total + terms[v, k].astype(jnp.float32)
        summed[v] = total
        sent[v] = total.astype(jnp.bfloat16)
        push(sent.at[v], crossed.at[v], cross_send.at[v], cross_recv.at[v], mirror)

    def finish(v):
        await_bytes(crossed.at[v], cross_recv.at[v])
        total = summed[v] + crossed[v].astype(jnp.float32)
        factor = 2.0 * LAMBDA / images
        mix[v, owned_rows(place)] = (total * factor).astype(jnp.bfloat16)
        each_near(lambda offset, other: push(
            mix.at[v, owned_rows(place)], mix.at[v, owned_rows(place)], ag_send.at[v], ag_recv.at[v], base + other))

    def self_weight(c):
        first, second = norm[0, c].astype(jnp.float32), norm[1, c].astype(jnp.float32)
        diagonal = jnp.sum(first * second, axis=0, keepdims=True) / images
        weight[c] = -2.0 * (1.0 - diagonal) - 2.0 * LAMBDA * diagonal

    def await_mix(v):
        await_bytes(mix.at[v, pl.ds(0, images - owned)], ag_recv.at[v])

    def backward(v, c):
        floats = norm[v, c].astype(jnp.float32)
        dnorm = jnp.dot(mix[1 - v], norm[v, c], preferred_element_type=jnp.float32)
        dnorm = dnorm + norm[1 - v, c].astype(jnp.float32) * weight[c]
        mean_d = jnp.mean(dnorm, axis=0, keepdims=True)
        mean_p = jnp.mean(dnorm * floats, axis=0, keepdims=True)
        grad[v, c] = ((dnorm - mean_d - floats * mean_p) * inv[v, c]).astype(jnp.bfloat16)
        copy = pltpu.make_async_copy(grad.at[v, c, my_rows(me)], outs[v].at[:, columns(me, c)], own_sem.at[v, c])
        copy.start()
        return copy

    copies = []
    send_view(0, 0)
    send_view(0, 1)
    send_view(1, 0, 0)
    send_view(1, 0, 1)
    normalize(0, 0)
    inner(0, 0)
    normalize(0, 1)
    inner(0, 1)
    send_view(1, 0, 2)
    send_view(1, 0, 3)
    send_view(1, 1, 0)
    reduce(0)
    send_view(1, 1, 1)
    send_view(1, 1, 2)
    finish(0)
    send_view(1, 1, 3)
    normalize(1, 0)
    inner(1, 0)
    self_weight(0)
    await_mix(0)
    copies.append(backward(1, 0))
    send_grad(1, 0, 0)
    normalize(1, 1)
    inner(1, 1)
    send_grad(1, 0, 1)
    send_grad(1, 0, 2)
    self_weight(1)
    reduce(1)
    send_grad(1, 0, 3)
    copies.append(backward(1, 1))
    send_grad(1, 1, 0)
    finish(1)
    send_grad(1, 1, 1)
    send_grad(1, 1, 2)
    send_grad(1, 1, 3)
    await_mix(1)
    for c in range(chunks):
        copies.append(backward(0, c))
        send_grad(0, c)

    for copy in copies:
        copy.wait()
    for v in range(2):
        await_bytes(terms.at[v], rs_send.at[v])
        await_bytes(sent.at[v], cross_send.at[v])
        await_bytes(mix.at[v, pl.ds(0, images - owned)], ag_send.at[v])
        for c in range(chunks):
            await_bytes(recv.at[v, c, pl.ds(0, images - rows)], in_send.at[v, c])
            await_bytes(grad.at[v, c, pl.ds(0, images - rows)], out_send.at[v, c])
            await_bytes(grad.at[v, c, pl.ds(0, images - rows)], out_recv.at[v, c])


def body(n, view_a, view_b):
    rows, features = view_a.shape
    images, width = rows * n, features // n
    chunks = CHUNKS
    while width % (chunks * 128):
        chunks -= 1
    step = width // chunks
    half = jnp.bfloat16
    blocks = (2, chunks, images, step)
    return pl.pallas_call(
        functools.partial(kernel, n, chunks),
        out_shape=[jax.ShapeDtypeStruct(view_a.shape, half)] * 2,
        in_specs=[pl.BlockSpec(memory_space=pltpu.HBM)] * 2,
        out_specs=[pl.BlockSpec(memory_space=pl.ANY)] * 2,
        scratch_shapes=[
            pltpu.VMEM(blocks, half),
            pltpu.VMEM(blocks, half),
            pltpu.VMEM((2, chunks, 1, step), jnp.float32),
            pltpu.VMEM((chunks, 1, step), jnp.float32),
            pltpu.VMEM((images, images), jnp.float32),
            pltpu.VMEM((2, images, images), half),
            pltpu.VMEM((2, n // 2 - 1, 2 * rows, images), half),
            pltpu.VMEM((2, 2 * rows, images), jnp.float32),
            pltpu.VMEM((2, 2 * rows, images), half),
            pltpu.VMEM((2, 2 * rows, images), half),
            pltpu.VMEM((2, images, images), half),
            pltpu.VMEM(blocks, half),
            pltpu.SemaphoreType.DMA((2, chunks)),
            pltpu.SemaphoreType.DMA((2, chunks)),
            pltpu.SemaphoreType.DMA((2, chunks)),
            pltpu.SemaphoreType.DMA((2,)),
            pltpu.SemaphoreType.DMA((2,)),
            pltpu.SemaphoreType.DMA((2,)),
            pltpu.SemaphoreType.DMA((2,)),
            pltpu.SemaphoreType.DMA((2,)),
            pltpu.SemaphoreType.DMA((2,)),
            pltpu.SemaphoreType.DMA((2, chunks)),
            pltpu.SemaphoreType.DMA((2, chunks)),
        ],
        compiler_params=pltpu.CompilerParams(
            collective_id=0, has_side_effects=True, vmem_limit_bytes=48 * 1024 * 1024),
        cost_estimate=pl.CostEstimate(
            flops=8 * images * images * width, bytes_accessed=8 * rows * features, transcendentals=2 * width),
    )(view_a, view_b)


def solution(mesh):
    placed = (P(("rep", "feat"), None), P(("rep", "feat"), None))
    return jax.shard_map(
        functools.partial(body, mesh.shape["feat"]),
        mesh=mesh,
        in_specs=placed,
        out_specs=placed,
        check_vma=False,
    )
```
